128 devices in a mesh: vid: 16 (over z, y), aud: 8 (over x, core).
Axes of the slice: x: 4, y: 4, z: 4, core: 2. Of those that a mesh axis runs over, the one named last changes fastest.
Arguments:
- video_q: bfloat16 [65536, 2048], P('vid', 'aud'), may hold values from -6 to 6
- video_k: bfloat16 [65536, 2048], P('vid', 'aud'), may hold values from -6 to 6
- video_v: bfloat16 [65536, 2048], P('vid', 'aud'), may hold values from -6 to 6
- video_dout: bfloat16 [65536, 2048], P('vid', 'aud'), may hold values from -6 to 6
- audio_q: bfloat16 [16384, 2048], P(('vid', 'aud')), may hold values from -6 to 6
- audio_k: bfloat16 [16384, 2048], P(('vid', 'aud')), may hold values from -6 to 6
- audio_v: bfloat16 [16384, 2048], P(('vid', 'aud')), may hold values from -6 to 6
- audio_dout: bfloat16 [16384, 2048], P(('vid', 'aud')), may hold values from -6 to 6
- video_pairs: int32 [128, 8], replicated, may hold values from 0 to 127, as said below
- audio_pairs: int32 [128, 8], replicated, may hold values from 0 to 127, as said below
- video_len: int32 [128], replicated, may hold values from 64 to 512
- audio_len: int32 [128], replicated, may hold values from 16 to 128
Outputs:
- video_out: bfloat16 [65536, 2048], P('vid', 'aud')
- audio_out: bfloat16 [16384, 2048], P(('vid', 'aud'))
- video_dq: bfloat16 [65536, 2048], P('vid', 'aud')
- video_dk: bfloat16 [65536, 2048], P('vid', 'aud')
- video_dv: bfloat16 [65536, 2048], P('vid', 'aud')
- audio_dq: bfloat16 [16384, 2048], P(('vid', 'aud'))
- audio_dk: bfloat16 [16384, 2048], P(('vid', 'aud'))
- audio_dv: bfloat16 [16384, 2048], P(('vid', 'aud'))
The draws below stay inside these ranges and needn't reach their ends.
Inputs may be any that keep to these rules, and one draw needn't show every extreme that they name: `video_pairs`: row b lists 8 consecutive audio blocks in increasing order, block b among them. `audio_pairs`: row b lists 8 consecutive video blocks in increasing order, block b among them.
All inputs are finite; a program needn't handle non-finite values.
Results may differ from the reference program's by a relative error of at most 0.024.
Values may be sent and summed in bfloat16 or wider, within the bound.
No kernel may reach another device: no remote copies, remote signals or barrier semaphores. Data moves between devices by JAX's collectives and lax.ppermute only.
A program may use at most 256 MiB of HBM per device.

```python
import math
import jax
import jax.numpy as jnp
from jax import lax

HEADS = 16
DH = 128
BV = 512
BA = 128
P_SIZE = 8
NB = 128
TV = 65536
TA = 16384
HD = 2048


def drawn_field(key, block):
    return jnp.clip(jax.random.normal(key, (NB, block, HEADS, DH), jnp.float32), -6.0, 6.0)


def draw_video_q(key, part):
    key = jax.random.fold_in(key, 1)
    field = drawn_field(key, BV)
    return field.reshape(NB * BV, HEADS * DH).astype(jnp.bfloat16)


def draw_audio_k(key, part):
    key = jax.random.fold_in(key, 2)
    field = drawn_field(key, BA)
    return field.reshape(NB * BA, HEADS * DH).astype(jnp.bfloat16)


def draw_audio_q(key, part):
    key = jax.random.fold_in(key, 3)
    field = drawn_field(key, BA)
    return field.reshape(NB * BA, HEADS * DH).astype(jnp.bfloat16)


def draw_video_k(key, part):
    key = jax.random.fold_in(key, 4)
    field = drawn_field(key, BV)
    return field.reshape(NB * BV, HEADS * DH).astype(jnp.bfloat16)


def block_lists(key):
    offset = jax.random.randint(key, (NB,), -(P_SIZE - 1), 1, dtype=jnp.int32)
    first_block = jnp.clip(jnp.arange(NB, dtype=jnp.int32) + offset, 0, NB - P_SIZE)
    return first_block[:, None] + jnp.arange(P_SIZE, dtype=jnp.int32)[None, :]


def draw_video_pairs(key, part):
    key = jax.random.fold_in(key, 5)
    return block_lists(key)


def draw_audio_pairs(key, part):
    key = jax.random.fold_in(key, 6)
    return block_lists(key)


def place_ends(array, stream_key, low, high):
    longest = array.shape.index(max(array.shape))
    spots = []
    for shift in (0, 1):
        where = [jax.random.randint(jax.random.fold_in(stream_key, axis), (), 0, length) for axis, length in enumerate(array.shape)]
        where[longest] = (where[longest] + shift) % array.shape[longest]
        spots.append(tuple(where))
    return array.at[spots[0]].set(low).at[spots[1]].set(high)


def steps_of(rng, extent, shards, least, high):
    def one(position, parts):
        steps = jax.random.uniform(jax.random.fold_in(jax.random.fold_in(rng, 6), position), (parts,), jnp.float32, least / len(shards), high / len(shards))
        return jnp.repeat(jnp.exp(steps), extent[position] // parts).reshape((-1,) + (1,) * (len(extent) - position - 1))

    factor_of = one(*shards[0])
    for cut in shards[1:]:
        factor_of = factor_of * one(*cut)
    return factor_of


def scatter_about(stream_key, dims, spread, limit, cuts=(), kind=jnp.bfloat16):
    drawn = jax.random.normal(stream_key, dims, jnp.float32) * spread
    if len(cuts) > 0:
        drawn = steps_of(stream_key, dims, cuts, -0.22, 0.18) * drawn
    return jnp.clip(drawn, min=-limit, max=limit).astype(kind)


def setup_inputs(seed: int = 0) -> dict:
    splits = jax.random.split(jax.random.key(seed), 13)
    return {
        "video_q": draw_video_q(jax.random.fold_in(splits[12], 71), 0),
        "video_k": draw_video_k(jax.random.fold_in(splits[12], 71), 0),
        "video_v": scatter_about(splits[2], (TV, HD), 1.0, 6.0, ((0, 16), (1, 8))),
        "video_dout": scatter_about(splits[3], (TV, HD), 1.0, 6.0, ((0, 16), (1, 8))),
        "audio_q": draw_audio_q(jax.random.fold_in(splits[12], 71), 0),
        "audio_k": draw_audio_k(jax.random.fold_in(splits[12], 71), 0),
        "audio_v": scatter_about(splits[6], (TA, HD), 1.0, 6.0, ((0, 128),)),
        "audio_dout": scatter_about(splits[7], (TA, HD), 1.0, 6.0, ((0, 128),)),
        "video_pairs": draw_video_pairs(jax.random.fold_in(splits[12], 71), 0),
        "audio_pairs": draw_audio_pairs(jax.random.fold_in(splits[12], 71), 0),
        "video_len": place_ends(jax.random.randint(splits[10], (NB,), max(2, BV // 8), BV + 1), jax.random.fold_in(splits[10], 1), max(2, BV // 8), BV).astype(jnp.int32),
        "audio_len": place_ends(jax.random.randint(splits[11], (NB,), max(2, BA // 8), BA + 1), jax.random.fold_in(splits[11], 1), max(2, BA // 8), BA).astype(jnp.int32),
    }


NEG_FILL = -1e+30

def attend_block(queries, keys, values, grad_out, key_valid):
    highest = lax.Precision.HIGHEST
    inv_root = 1.0 / math.sqrt(queries.shape[-1])
    query_wide = queries.astype(jnp.float32)
    key_wide = keys.astype(jnp.float32)
    value_wide = values.astype(jnp.float32)
    grad_wide = grad_out.astype(jnp.float32)
    scores = jnp.einsum('rge,kge->grk', query_wide, key_wide, precision=highest) * inv_root
    scores = jnp.where(key_valid, scores, NEG_FILL)
    row_top = lax.optimization_barrier(jnp.max(scores, axis=2, keepdims=True))
    exponent = jnp.where(key_valid, jnp.exp(scores - row_top), 0.0)
    weights = exponent / lax.optimization_barrier(jnp.sum(exponent, axis=2, keepdims=True))
    weights_half = lax.optimization_barrier(weights.astype(jnp.bfloat16)).astype(jnp.float32)
    outputs = jnp.einsum('grk,kge->rge', weights_half, value_wide, precision=highest)
    dprob = jnp.einsum('rge,kge->grk', grad_wide, value_wide, precision=highest)
    delta_sum = lax.optimization_barrier(jnp.sum(weights * dprob, axis=2, keepdims=True))
    dscore = lax.optimization_barrier((weights * (dprob - delta_sum)).astype(jnp.bfloat16)).astype(jnp.float32)
    query_grad = jnp.einsum('grk,kge->rge', dscore, key_wide, precision=highest) * inv_root
    key_grad = jnp.einsum('grk,rge->kge', dscore, query_wide, precision=highest) * inv_root
    value_grad = jnp.einsum('grk,rge->kge', weights_half, grad_wide, precision=highest)
    return (outputs, query_grad, key_grad, value_grad)

def cross_direction(queries, keys, values, grad_out, pairs, key_len, block_q, block_k):
    blocks = queries.shape[0] // block_q
    feature_width = queries.shape[1]
    heads_count = feature_width // DH
    offsets = jnp.arange(block_k, dtype=jnp.int32)

    def one_block(carry, index):
        key_acc, value_acc = carry
        listed = pairs[index]
        key_rows = (listed[:, None] * block_k + offsets[None, :]).reshape(-1)
        key_valid = (offsets[None, :] < key_len[listed][:, None]).reshape(1, 1, -1)
        start = (index * block_q).astype(jnp.int32)
        query_rows = lax.dynamic_slice_in_dim(queries, start, block_q, 0).reshape(block_q, heads_count, DH)
        grad_rows = lax.dynamic_slice_in_dim(grad_out, start, block_q, 0).reshape(block_q, heads_count, DH)
        key_tile = keys[key_rows].reshape(-1, heads_count, DH)
        value_tile = values[key_rows].reshape(-1, heads_count, DH)
        outputs, query_grad, key_grad, value_grad = attend_block(query_rows, key_tile, value_tile, grad_rows, key_valid)
        key_acc = key_acc.at[key_rows].add(key_grad.reshape(-1, feature_width))
        value_acc = value_acc.at[key_rows].add(value_grad.reshape(-1, feature_width))
        return ((key_acc, value_acc), (outputs.reshape(block_q, feature_width).astype(jnp.bfloat16), query_grad.reshape(block_q, feature_width).astype(jnp.bfloat16)))
    zeros_acc = jnp.zeros((keys.shape[0], feature_width), jnp.float32)
    (key_acc, value_acc), (outputs, query_grad) = lax.scan(one_block, (zeros_acc, zeros_acc), jnp.arange(blocks, dtype=jnp.int32))
    return (outputs.reshape(-1, feature_width), query_grad.reshape(-1, feature_width), key_acc.astype(jnp.bfloat16), value_acc.astype(jnp.bfloat16))

def reference(video_q, video_k, video_v, video_dout, audio_q, audio_k, audio_v, audio_dout, video_pairs, audio_pairs, video_len, audio_len):
    video_out, video_dq, audio_dk, audio_dv = cross_direction(video_q, audio_k, audio_v, video_dout, video_pairs, audio_len, BV, BA)
    audio_out, audio_dq, video_dk, video_dv = cross_direction(audio_q, video_k, video_v, audio_dout, audio_pairs, video_len, BA, BV)
    return (video_out, audio_out, video_dq, video_dk, video_dv, audio_dq, audio_dk, audio_dv)
```

```python
import functools
import math

import jax
import jax.numpy as jnp
from jax import lax
from jax.experimental import pallas as pl
from jax.experimental.pallas import tpu as pltpu
from jax.sharding import PartitionSpec as P

DH = 128
BV = 512
BA = 128
P_SIZE = 8
NB = 128
SPAN = 8
REACH = P_SIZE - 1
EXT = SPAN + 2 * REACH
WIDE = 2 * DH
NEG = -1e30
INV_ROOT = 1.0 / math.sqrt(DH)
C2 = math.log2(math.e) / math.sqrt(DH)
F32 = jnp.float32
BF16 = jnp.bfloat16
MIB = 1024 * 1024
PACK = 16
GROUP_FORMS = (5, 6, 8)
VIDEO_ROWS = SPAN * BV
AUDIO_ROWS = EXT * BA


def dot_nt(a, b):
    return lax.dot_general(a, b, (((1,), (1,)), ((), ())), preferred_element_type=F32)


def dot_nn(a, b):
    return jnp.dot(a, b, preferred_element_type=F32)


def split_rows(column0, column1, rows):
    return jnp.concatenate(
        [jnp.broadcast_to(column0, (rows, DH)), jnp.broadcast_to(column1, (rows, DH))], axis=1
    )


def put_diagonal(ref, tile):
    ref[0:DH, 0:DH] = tile[:, 0:DH]
    ref[DH:WIDE, DH:WIDE] = tile[:, DH:WIDE]


def clear_corners(ref):
    ref[0:DH, DH:WIDE] = jnp.zeros((DH, DH), ref.dtype)
    ref[DH:WIDE, 0:DH] = jnp.zeros((DH, DH), ref.dtype)


def padded(length):
    return (length + PACK - 1) // PACK * PACK


def aligned(row):
    return pl.multiple_of(row, PACK)


def pick(cond, value, other):
    return jnp.where(cond, value, other)


def block_row(count, width):
    return lax.broadcasted_iota(jnp.int32, (count, width), 0)


def global_block(first, e):
    return jnp.clip(first - REACH + e, 0, NB - 1)


def pack_kernel(first_ref, len_ref, k_ref, v_ref, kc_ref, vc_ref):
    first = first_ref[0]
    row = block_row(BV, WIDE)
    zeros = jnp.zeros((BV, WIDE), BF16)

    def one(c, offset):
        length = len_ref[first + c]
        rows = pl.ds(aligned(offset), BV)
        kc_ref[rows, :] = pick(row < length, k_ref[c], zeros)
        vc_ref[rows, :] = pick(row < length, v_ref[c], zeros)
        return offset + padded(length)

    end = lax.fori_loop(0, SPAN, one, 0)
    rows = pl.ds(aligned(end), BV)
    kc_ref[rows, :] = zeros
    vc_ref[rows, :] = zeros


def run_pack(first, lengths, k, v):
    shape = (VIDEO_ROWS + BV, WIDE)
    return pl.pallas_call(
        pack_kernel,
        grid_spec=pltpu.PrefetchScalarGridSpec(
            num_scalar_prefetch=2,
            grid=(1,),
            in_specs=[whole(k.shape), whole(v.shape)],
            out_specs=[whole(shape), whole(shape)],
        ),
        out_shape=[jax.ShapeDtypeStruct(shape, BF16)] * 2,
        compiler_params=pltpu.CompilerParams(vmem_limit_bytes=12 * MIB),
        cost_estimate=pl.CostEstimate(
            flops=1_000_000_000, bytes_accessed=20_000_000, transcendentals=0
        ),
        name="pack_video",
    )(first, lengths, k, v)


def video_kernel(
    first_ref,
    pairs_ref,
    len_ref,
    q_ref,
    do_ref,
    before_ref,
    own_ref,
    after_ref,
    out_ref,
    dq_ref,
    gbefore_ref,
    gown_ref,
    gafter_ref,
    kc,
    vc,
    bias,
    dk_acc,
    dv_acc,
    kbd,
    vbd,
    s_scr,
    p_scr,
    offsets,
):
    j = pl.program_id(0)
    first = first_ref[0]
    sources = (
        (before_ref, gbefore_ref, 0, REACH),
        (own_ref, gown_ref, REACH, SPAN),
        (after_ref, gafter_ref, REACH + SPAN, REACH),
    )
    row = block_row(BA, WIDE)
    narrow_row = block_row(BA, BA)

    @pl.when(j == 0)
    def _():
        for i in range(P_SIZE):
            clear_corners(kbd.at[i])
            clear_corners(vbd.at[i])

        def clear(i, carry):
            rows = pl.ds(i * BA, BA)
            kc[rows, :] = jnp.zeros((BA, WIDE), BF16)
            vc[rows, :] = jnp.zeros((BA, WIDE), BF16)
            bias[rows, :] = jnp.full((BA, BA), NEG, F32)
            dk_acc[rows, :] = jnp.zeros((BA, WIDE), F32)
            dv_acc[rows, :] = jnp.zeros((BA, WIDE), F32)
            return carry

        lax.fori_loop(0, EXT + 1, clear, 0)
        offset = jnp.int32(0)
        for source, _, base, count in sources:

            def one(i, offset, source=source, base=base):
                length = len_ref[global_block(first, base + i)]
                rows = pl.ds(aligned(offset), BA)
                offsets[base + i] = offset
                kc[rows, :] = pick(row < length, source[i, 0], jnp.zeros((BA, WIDE), BF16))
                vc[rows, :] = pick(row < length, source[i, 1], jnp.zeros((BA, WIDE), BF16))
                bias[rows, :] = pick(narrow_row < length, 0.0, NEG)
                return offset + padded(length)

            offset = lax.fori_loop(0, count, one, offset)
        offsets[EXT] = offset

    start = pairs_ref[first + j, 0]
    e = start - first + REACH
    low = offsets[e]
    high = offsets[e + P_SIZE]
    groups = (high - low + BA - 1) // BA
    place = lax.broadcasted_iota(jnp.int32, (BA, BA), 1)

    def attend(count):
        q = q_ref[...]
        do = do_ref[...]
        spots = []
        for i in range(count):
            begin = jnp.minimum(low + i * BA, AUDIO_ROWS)
            rows = pl.ds(aligned(begin), BA)
            spots.append(rows)
            put_diagonal(kbd.at[i], kc[rows, :])
            put_diagonal(vbd.at[i], vc[rows, :])
        top = None
        for i in range(count):
            begin = jnp.minimum(low + i * BA, AUDIO_ROWS)
            shut = pick(place < high - begin, bias[spots[i], :].T, NEG)[0:1, :]
            s = dot_nt(q, kbd[i]) + jnp.concatenate([shut, shut], axis=1)
            s_scr[i] = s
            top = s if top is None else jnp.maximum(top, s)
        peak = C2 * split_rows(
            jnp.max(top[:, 0:DH], axis=1, keepdims=True),
            jnp.max(top[:, DH:WIDE], axis=1, keepdims=True),
            BV,
        )
        total = None
        acc = None
        for i in range(count):
            ex = jnp.exp2(s_scr[i] * C2 - peak)
            total = ex if total is None else total + ex
            p = ex.astype(BF16)
            p_scr[i] = p
            part = dot_nn(p, vbd[i])
            acc = part if acc is None else acc + part
        scale = 1.0 / split_rows(
            jnp.sum(total[:, 0:DH], axis=1, keepdims=True),
            jnp.sum(total[:, DH:WIDE], axis=1, keepdims=True),
            BV,
        )
        out = acc * scale
        out_ref[...] = out.astype(BF16)
        do_wide = do.astype(F32)
        prod = do_wide * out
        delta = split_rows(
            jnp.sum(prod[:, 0:DH], axis=1, keepdims=True),
            jnp.sum(prod[:, DH:WIDE], axis=1, keepdims=True),
            BV,
        )
        scale_in = scale * INV_ROOT
        q_t = (q.astype(F32) * scale_in).astype(BF16).T
        do_t = (do_wide * scale).astype(BF16).T
        acc = None
        for i in range(count):
            dp = dot_nt(do, vbd[i])
            p = p_scr[i]
            ds = (p.astype(F32) * (dp - delta)).astype(BF16)
            part = dot_nn(ds, kbd[i])
            acc = part if acc is None else acc + part
            for h in range(2):
                cut = slice(h * DH, (h + 1) * DH)
                dk_acc[spots[i], cut] += dot_nn(q_t[cut, :], ds[:, cut]).T
                dv_acc[spots[i], cut] += dot_nn(do_t[cut, :], p[:, cut]).T
        dq_ref[...] = (acc * scale_in).astype(BF16)

    below = 0
    for count in GROUP_FORMS:
        pl.when(jnp.logical_and(groups > below, groups <= count))(functools.partial(attend, count))
        below = count

    @pl.when(j == pl.num_programs(0) - 1)
    def _():
        for _, target, base, count in sources:

            def one(i, carry, target=target, base=base):
                length = len_ref[global_block(first, base + i)]
                rows = pl.ds(aligned(offsets[base + i]), BA)
                target[i, 0] = pick(row < length, dk_acc[rows, :], 0.0).astype(target.dtype)
                target[i, 1] = pick(row < length, dv_acc[rows, :], 0.0).astype(target.dtype)
                return carry

            lax.fori_loop(0, count, one, 0)


def whole(shape):
    return pl.BlockSpec(shape, lambda *_: (0,) * len(shape), pipeline_mode=pl.Buffered(1))


def run_video(first, pairs, lengths, q, do, before, own, after):
    rows = pl.BlockSpec((BV, WIDE), lambda j, *_: (j, 0))
    return pl.pallas_call(
        video_kernel,
        grid_spec=pltpu.PrefetchScalarGridSpec(
            num_scalar_prefetch=3,
            grid=(SPAN,),
            in_specs=[rows, rows, whole(before.shape), whole(own.shape), whole(after.shape)],
            out_specs=[rows, rows, whole(before.shape), whole(own.shape), whole(after.shape)],
            scratch_shapes=[
                pltpu.VMEM((AUDIO_ROWS + BA, WIDE), BF16),
                pltpu.VMEM((AUDIO_ROWS + BA, WIDE), BF16),
                pltpu.VMEM((AUDIO_ROWS + BA, BA), F32),
                pltpu.VMEM((AUDIO_ROWS + BA, WIDE), F32),
                pltpu.VMEM((AUDIO_ROWS + BA, WIDE), F32),
                pltpu.VMEM((P_SIZE, WIDE, WIDE), BF16),
                pltpu.VMEM((P_SIZE, WIDE, WIDE), BF16),
                pltpu.VMEM((P_SIZE, BV, WIDE), F32),
                pltpu.VMEM((P_SIZE, BV, WIDE), BF16),
                pltpu.SMEM((32,), jnp.int32),
            ],
        ),
        out_shape=[
            jax.ShapeDtypeStruct(q.shape, BF16),
            jax.ShapeDtypeStruct(q.shape, BF16),
            jax.ShapeDtypeStruct(before.shape, BF16),
            jax.ShapeDtypeStruct(own.shape, F32),
            jax.ShapeDtypeStruct(after.shape, BF16),
        ],
        compiler_params=pltpu.CompilerParams(vmem_limit_bytes=32 * MIB),
        cost_estimate=pl.CostEstimate(
            flops=20_000_000_000, bytes_accessed=20_000_000, transcendentals=8_000_000
        ),
        name="video_queries",
    )(first, pairs, lengths, q, do, before, own, after)


def packed_range(first, pairs_ref, offsets, block):
    inside = jnp.logical_and(block >= 0, block < NB)
    start = pairs_ref[jnp.clip(block, 0, NB - 1), 0] - first
    low = offsets[jnp.clip(start, 0, SPAN)]
    high = offsets[jnp.clip(start + P_SIZE, 0, SPAN)]
    return low, pick(inside, high, low)


def fill_bias(first, len_ref, bias, offsets):
    row = block_row(BV, BA)

    def one(c, offset):
        length = len_ref[first + c]
        offsets[c] = offset
        bias[pl.ds(aligned(offset), BV), :] = pick(row < length, 0.0, NEG)
        return offset + padded(length)

    end = lax.fori_loop(0, SPAN, one, 0)
    offsets[SPAN] = end
    bias[pl.ds(aligned(end), BV), :] = jnp.full((BV, BA), NEG, F32)


def part_kernel(pieces, first_ref, pairs_ref, len_ref, *refs):
    sources = refs[: len(pieces)]
    kc_ref, vc_ref, o_ref, st_ref, qbd, s_scr, bias, offsets = refs[len(pieces) :]
    b = pl.program_id(0)
    first = first_ref[0]

    @pl.when(b == 0)
    def _():
        clear_corners(qbd)
        fill_bias(first, len_ref, bias, offsets)

    block = first
    for base, begin, count in pieces:
        inside = jnp.logical_and(b >= begin, b < begin + count)
        block = pick(inside, first + base + b - begin, block)
    low, high = packed_range(first, pairs_ref, offsets, block)
    chunks = (high - low + BV - 1) // BV
    row = block_row(BV, BA)

    @pl.when(chunks == 0)
    def _():
        o_ref[0] = jnp.zeros((WIDE, BA), F32)
        st_ref[0, 0:1, :] = jnp.full((1, WIDE), NEG, F32)
        st_ref[0, 1:2, :] = jnp.zeros((1, WIDE), F32)

    for (_, begin, count), source in zip(pieces, sources):

        @pl.when(jnp.logical_and(chunks > 0, jnp.logical_and(b >= begin, b < begin + count)))
        def _(source=source, begin=begin):
            put_diagonal(qbd, source[b - begin, 0])

    def attend(count):
        spots = [aligned(low + i * BV) for i in range(count)]
        peak = None
        for i, spot in enumerate(spots):
            rows = pl.ds(spot, BV)
            shut = bias[rows, :]
            if i == count - 1:
                shut = pick(row < high - spot, shut, NEG)
            s = dot_nt(kc_ref[rows, :], qbd[...]) + jnp.concatenate([shut, shut], axis=1)
            s_scr[i] = s
            top = jnp.max(s, axis=0, keepdims=True)
            peak = top if peak is None else jnp.maximum(peak, top)
        peak = peak * C2
        total = None
        acc = [None, None]
        for i, spot in enumerate(spots):
            ex = jnp.exp2(s_scr[i] * C2 - peak)
            part = jnp.sum(ex, axis=0, keepdims=True)
            total = part if total is None else total + part
            p = ex.astype(BF16)
            v_t = vc_ref[pl.ds(spot, BV), :].T
            for h in range(2):
                cut = slice(h * DH, (h + 1) * DH)
                part = dot_nn(v_t[cut, :], p[:, cut])
                acc[h] = part if acc[h] is None else acc[h] + part
        scale = 1.0 / total
        st_ref[0, 0:1, :] = peak + jnp.log2(total)
        for h in range(2):
            cut = slice(h * DH, (h + 1) * DH)
            o_ref[0, cut, :] = acc[h] * scale[:, cut]

    for count in range(1, SPAN + 1):
        pl.when(chunks == count)(functools.partial(attend, count))

    for (_, begin, count), source in zip(pieces, sources):

        @pl.when(jnp.logical_and(chunks > 0, jnp.logical_and(b >= begin, b < begin + count)))
        def _(source=source, begin=begin):
            for h in range(2):
                cut = slice(h * DH, (h + 1) * DH)
                do_t = source[b - begin, 1, :, cut].T.astype(F32)
                st_ref[0, 1:2, cut] = jnp.sum(o_ref[0, cut, :] * do_t, axis=0, keepdims=True)


def run_part(pieces, first, pairs, lengths, sources, kc, vc):
    count = sum(piece[2] for piece in pieces)
    return pl.pallas_call(
        functools.partial(part_kernel, pieces),
        grid_spec=pltpu.PrefetchScalarGridSpec(
            num_scalar_prefetch=3,
            grid=(count,),
            in_specs=[whole(a.shape) for a in sources] + [whole(kc.shape), whole(vc.shape)],
            out_specs=[
                pl.BlockSpec((1, WIDE, BA), lambda b, *_: (b, 0, 0)),
                pl.BlockSpec((1, 8, WIDE), lambda b, *_: (b, 0, 0)),
            ],
            scratch_shapes=[
                pltpu.VMEM((WIDE, WIDE), BF16),
                pltpu.VMEM((SPAN, BV, WIDE), F32),
                pltpu.VMEM((VIDEO_ROWS + BV, BA), F32),
                pltpu.SMEM((16,), jnp.int32),
            ],
        ),
        out_shape=[
            jax.ShapeDtypeStruct((count, WIDE, BA), F32),
            jax.ShapeDtypeStruct((count, 8, WIDE), F32),
        ],
        compiler_params=pltpu.CompilerParams(vmem_limit_bytes=18 * MIB),
        cost_estimate=pl.CostEstimate(
            flops=8_000_000_000, bytes_accessed=6_000_000, transcendentals=count * 500_000
        ),
        name="audio_parts",
    )(first, pairs, lengths, *sources, kc, vc)


def grad_kernel(pieces, last, first_ref, pairs_ref, len_ref, *refs):
    n = len(pieces)
    sources = refs[:n]
    rest = refs[n:]
    st_ref, above_ref, below_ref, o_ref, kc_ref, vc_ref = rest[:6]
    rest = rest[6:]
    if last:
        dk_in, dv_in = rest[:2]
        rest = rest[2:]
    targets = rest[:n]
    dk_ref, dv_ref, qbd, dobd, acc, bias, offsets = rest[n : n + 7]
    if last:
        dk_acc, dv_acc = rest[n + 7 :]
    else:
        dk_acc, dv_acc = dk_ref, dv_ref
    b = pl.program_id(0)
    first = first_ref[0]

    @pl.when(b == 0)
    def _():
        clear_corners(qbd)
        clear_corners(dobd)
        fill_bias(first, len_ref, bias, offsets)

        def clear(c, carry):
            rows = pl.ds(pl.multiple_of(c * BV, BV), BV)
            dk_acc[rows, :] = dk_in[rows, :] if last else jnp.zeros((BV, WIDE), F32)
            dv_acc[rows, :] = dv_in[rows, :] if last else jnp.zeros((BV, WIDE), F32)
            return carry

        lax.fori_loop(0, SPAN + 1, clear, 0)

    block = first
    for base, begin, count in pieces:
        inside = jnp.logical_and(b >= begin, b < begin + count)
        block = pick(inside, first + base + b - begin, block)
    low, high = packed_range(first, pairs_ref, offsets, block)
    chunks = (high - low + BV - 1) // BV
    row = block_row(BV, BA)
    for (_, begin, count), source, target in zip(pieces, sources, targets):
        inside = jnp.logical_and(b >= begin, b < begin + count)

        @pl.when(jnp.logical_and(chunks > 0, inside))
        def _(source=source, begin=begin):
            put_diagonal(qbd, source[b - begin, 0])
            put_diagonal(dobd, source[b - begin, 1])

        @pl.when(jnp.logical_and(chunks == 0, inside))
        def _(target=target, begin=begin):
            target[b - begin] = jnp.zeros((2, BA, WIDE), target.dtype)

    mine = st_ref[b]
    if last:
        above = above_ref[REACH + jnp.maximum(b - 1, 0)]
        below = below_ref[REACH + jnp.minimum(b, REACH - 1)]
        logs = [
            mine[0:1],
            pick(b >= 1, above[0:1], NEG),
            pick(b < REACH, below[0:1], NEG),
        ]
        parts = [mine[1:2], above[1:2], below[1:2]]
    else:
        is_before = b < REACH
        slot = pick(is_before, b, b - REACH)
        other = pick(is_before, below_ref[slot], above_ref[slot])
        logs = [mine[0:1], other[0:1]]
        parts = [mine[1:2], other[1:2]]
    peak = functools.reduce(jnp.maximum, logs)
    log_total = peak + jnp.log2(sum(jnp.exp2(x - peak) for x in logs))
    shares = [jnp.exp2(x - log_total) for x in logs]
    delta = sum(x * y for x, y in zip(shares, parts))

    @pl.when(chunks > 0)
    def _():
        acc[...] = jnp.zeros((WIDE, BA), F32)

    def step(i, carry):
        begin = aligned(low + i * BV)
        rows = pl.ds(begin, BV)
        shut = pick(row < high - begin, bias[rows, :], NEG)
        k = kc_ref[rows, :]
        s = dot_nt(k, qbd[...])
        w = jnp.exp2(s * C2 - log_total + jnp.concatenate([shut, shut], axis=1))
        dp = dot_nt(vc_ref[rows, :], dobd[...])
        ds = (w * (dp - delta)).astype(BF16)
        w = w.astype(BF16)
        dv_acc[rows, :] += dot_nn(w, dobd[...])
        dk_acc[rows, :] += dot_nn(ds, qbd[...])
        k_t = k.T
        for h in range(2):
            cut = slice(h * DH, (h + 1) * DH)
            acc[cut, :] += dot_nn(k_t[cut, :], ds[:, cut])
        return carry

    lax.fori_loop(0, chunks, step, 0)
    for (_, begin, count), target in zip(pieces, targets):

        @pl.when(jnp.logical_and(chunks > 0, jnp.logical_and(b >= begin, b < begin + count)))
        def _(target=target, begin=begin):
            for h in range(2):
                cut = slice(h * DH, (h + 1) * DH)
                spread = (o_ref[0, cut, :] * shares[0][:, cut]).T
                target[b - begin, 0, :, cut] = spread.astype(target.dtype)
                target[b - begin, 1, :, cut] = (acc[cut, :].T * INV_ROOT).astype(target.dtype)

    if last:

        @pl.when(b == pl.num_programs(0) - 1)
        def _():
            full_row = block_row(BV, WIDE)

            def drain(c, offset):
                length = len_ref[first + c]
                rows = pl.ds(aligned(offset), BV)
                valid = full_row < length
                dk_ref[c] = (pick(valid, dk_acc[rows, :], 0.0) * INV_ROOT).astype(BF16)
                dv_ref[c] = pick(valid, dv_acc[rows, :], 0.0).astype(BF16)
                return offset + padded(length)

            lax.fori_loop(0, SPAN, drain, 0)


def run_grad(pieces, last, first, pairs, lengths, sources, stats, above, below, o_t, kc, vc, accs):
    count = sum(piece[2] for piece in pieces)
    acc_shape = kc.shape
    grad_shape = (SPAN, BV, WIDE) if last else acc_shape
    target_shapes = [(piece[2], 2, BA, WIDE) for piece in pieces]
    operands = (*sources, stats, above, below, o_t, kc, vc, *accs)
    in_specs = [whole(a.shape) for a in operands]
    in_specs[len(sources) + 3] = pl.BlockSpec((1, WIDE, BA), lambda b, *_: (b, 0, 0))
    scratch = [
        pltpu.VMEM((WIDE, WIDE), BF16),
        pltpu.VMEM((WIDE, WIDE), BF16),
        pltpu.VMEM((WIDE, BA), F32),
        pltpu.VMEM((VIDEO_ROWS + BV, BA), F32),
        pltpu.SMEM((16,), jnp.int32),
    ]
    if last:
        scratch += [pltpu.VMEM(acc_shape, F32), pltpu.VMEM(acc_shape, F32)]
    return pl.pallas_call(
        functools.partial(grad_kernel, pieces, last),
        grid_spec=pltpu.PrefetchScalarGridSpec(
            num_scalar_prefetch=3,
            grid=(count,),
            in_specs=in_specs,
            out_specs=[whole(x) for x in target_shapes] + [whole(grad_shape)] * 2,
            scratch_shapes=scratch,
        ),
        out_shape=[jax.ShapeDtypeStruct(x, F32 if last else BF16) for x in target_shapes]
        + [jax.ShapeDtypeStruct(grad_shape, BF16 if last else F32)] * 2,
        compiler_params=pltpu.CompilerParams(vmem_limit_bytes=32 * MIB),
        cost_estimate=pl.CostEstimate(
            flops=10_000_000_000, bytes_accessed=20_000_000, transcendentals=4_000_000
        ),
        name="audio_gradients",
    )(first, pairs, lengths, *operands)


def routes(ring):
    size = lax.axis_size("vid")
    count = size if ring else size - 1
    up = [(i, (i + 1) % size) for i in range(count)]
    return up, [(j, i) for i, j in up]


def to_span(*arrays):
    tiles = jnp.stack([a.reshape(BA, 8, WIDE) for a in arrays], axis=1)
    tiles = jnp.transpose(tiles, (2, 1, 0, 3))
    return lax.all_to_all(tiles, "aud", split_axis=0, concat_axis=0, tiled=True)


def to_owner(tiles):
    back = lax.all_to_all(tiles, "aud", split_axis=0, concat_axis=0, tiled=True)
    return [jnp.transpose(back[:, i], (1, 0, 2)).reshape(BA, 8 * WIDE) for i in range(2)]


def halo(tiles):
    up, down = routes(False)
    return lax.ppermute(tiles[1:], "vid", up), lax.ppermute(tiles[:-1], "vid", down)


def give_back(before, after):
    up, down = routes(False)
    return lax.ppermute(before, "vid", down), lax.ppermute(after, "vid", up)


def spread_low(part):
    return jnp.pad(part, ((0, 1),) + ((0, 0),) * (part.ndim - 1))


def spread_high(part):
    return jnp.pad(part, ((1, 0),) + ((0, 0),) * (part.ndim - 1))


OWN = ((0, 0, SPAN),)
HALO = ((-REACH, 0, REACH), (SPAN, REACH, REACH))


def per_device(
    video_q,
    video_k,
    video_v,
    video_dout,
    audio_q,
    audio_k,
    audio_v,
    audio_dout,
    video_pairs,
    audio_pairs,
    video_len,
    audio_len,
):
    first = (lax.axis_index("vid") * SPAN).astype(jnp.int32).reshape(1)
    k = video_k.reshape(SPAN, BV, WIDE)
    v = video_v.reshape(SPAN, BV, WIDE)
    kc, vc = run_pack(first, video_len, k, v)
    qd = to_span(audio_q, audio_dout)
    qd, kc, vc = lax.optimization_barrier((qd, kc, vc))
    qd_before, qd_after = halo(qd)
    kv = to_span(audio_k, audio_v)
    kv_before, kv_after = halo(kv)

    o_own, st_own = run_part(OWN, first, audio_pairs, video_len, (qd,), kc, vc)
    near = (qd_before, qd_after)
    o_near, st_near = run_part(HALO, first, audio_pairs, video_len, near, kc, vc)
    up, down = routes(True)
    from_above = lax.ppermute(jnp.concatenate([st_own[:-1], st_near[:REACH]]), "vid", down)
    from_below = lax.ppermute(jnp.concatenate([st_own[1:], st_near[REACH:]]), "vid", up)

    video_out, video_dq, g_before, g_own, g_after = run_video(
        first, video_pairs, audio_len, video_q, video_dout, kv_before, kv, kv_after
    )
    g_above, g_below = give_back(g_before, g_after)

    od_before, od_after, dk_acc, dv_acc = run_grad(
        HALO, False, first, audio_pairs, video_len, near, st_near, from_above, from_below, o_near, kc, vc, ()
    )
    od_above, od_below = give_back(od_before, od_after)
    od_own, video_dk, video_dv = run_grad(
        OWN, True, first, audio_pairs, video_len, (qd,), st_own, from_above, from_below, o_own, kc, vc,
        (dk_acc, dv_acc),
    )

    g = (g_own + spread_high(g_above).astype(F32) + spread_low(g_below).astype(F32)).astype(BF16)
    audio_dk, audio_dv = to_owner(g)
    od = (od_own + spread_high(od_above).astype(F32) + spread_low(od_below).astype(F32)).astype(BF16)
    audio_out, audio_dq = to_owner(od)
    return (
        video_out,
        audio_out,
        video_dq,
        video_dk.reshape(video_k.shape),
        video_dv.reshape(video_k.shape),
        audio_dq,
        audio_dk,
        audio_dv,
    )


def solution(mesh):
    video = P("vid", "aud")
    audio = P(("vid", "aud"), None)
    return jax.shard_map(
        per_device,
        mesh=mesh,
        in_specs=(video,) * 4 + (audio,) * 4 + (P(),) * 4,
        out_specs=(video, audio, video, video, video, audio, audio, audio),
        check_vma=False,
    )
```

```python
import functools
import math

import jax
import jax.numpy as jnp
from jax import lax
from jax.experimental import pallas as pl
from jax.experimental.pallas import tpu as pltpu
from jax.sharding import PartitionSpec as P

DH = 128
BV = 512
BA = 128
P_SIZE = 8
NB = 128
SPAN = 8
REACH = P_SIZE - 1
EXT = SPAN + 2 * REACH
WIDE = 2 * DH
NEG = -1e30
INV_ROOT = 1.0 / math.sqrt(DH)
C2 = math.log2(math.e) / math.sqrt(DH)
F32 = jnp.float32
BF16 = jnp.bfloat16
MIB = 1024 * 1024
PACK = 16
OWN = ((0, 0, SPAN),)
HALO = ((-REACH, 0, REACH), (SPAN, REACH, REACH))
GROUP_FORMS = (4, 5, 6, 7, 8)
VIDEO_ROWS = SPAN * BV
AUDIO_ROWS = EXT * BA
NOTE = 16
LETTER = WIDE + 2 * NOTE


def dot_nt(a, b):
    return lax.dot_general(a, b, (((1,), (1,)), ((), ())), preferred_element_type=F32)


def dot_nn(a, b):
    return jnp.dot(a, b, preferred_element_type=F32)


def split_rows(column0, column1, rows):
    return jnp.concatenate(
        [jnp.broadcast_to(column0, (rows, DH)), jnp.broadcast_to(column1, (rows, DH))], axis=1
    )


def put_diagonal(ref, tile):
    ref[0:DH, 0:DH] = tile[:, 0:DH]
    ref[DH:WIDE, DH:WIDE] = tile[:, DH:WIDE]


def clear_corners(ref):
    ref[0:DH, DH:WIDE] = jnp.zeros((DH, DH), ref.dtype)
    ref[DH:WIDE, 0:DH] = jnp.zeros((DH, DH), ref.dtype)


def write_note(ref, i, row, stats):
    lines = []
    for stat in stats:
        for h in range(2):
            rest = stat[:, h * DH : (h + 1) * DH]
            for _ in range(3):
                piece = rest.astype(BF16)
                rest = rest - piece.astype(F32)
                lines.append(piece.astype(F32))
    lines.append(jnp.zeros((NOTE - len(lines), DH), F32))
    ref[i, row : row + NOTE, :] = jnp.concatenate(lines, axis=0).astype(BF16)


def read_note(ref, i, row):
    note = ref[i, row : row + NOTE, :].astype(F32)
    wide = []
    for k in range(4):
        wide.append(note[3 * k : 3 * k + 1] + note[3 * k + 1 : 3 * k + 2] + note[3 * k + 2 : 3 * k + 3])
    return (
        jnp.concatenate(wide[0:2], axis=1),
        jnp.concatenate(wide[2:4], axis=1),
    )


def padded(length):
    return (length + PACK - 1) // PACK * PACK


def aligned(row):
    return pl.multiple_of(row, PACK)


def pick(cond, value, other):
    return jnp.where(cond, value, other)


def block_row(count, width):
    return lax.broadcasted_iota(jnp.int32, (count, width), 0)


def global_block(first, e):
    return jnp.clip(first - REACH + e, 0, NB - 1)


def pack_kernel(first_ref, len_ref, k_ref, v_ref, kc_ref, vc_ref):
    first = first_ref[0]
    row = block_row(BV, WIDE)
    zeros = jnp.zeros((BV, WIDE), BF16)

    def one(c, offset):
        length = len_ref[first + c]
        rows = pl.ds(aligned(offset), BV)
        kc_ref[rows, :] = pick(row < length, k_ref[c], zeros)
        vc_ref[rows, :] = pick(row < length, v_ref[c], zeros)
        return offset + padded(length)

    end = lax.fori_loop(0, SPAN, one, 0)
    rows = pl.ds(aligned(end), BV)
    kc_ref[rows, :] = zeros
    vc_ref[rows, :] = zeros


def run_pack(first, lengths, k, v):
    shape = (VIDEO_ROWS + BV, WIDE)
    return pl.pallas_call(
        pack_kernel,
        grid_spec=pltpu.PrefetchScalarGridSpec(
            num_scalar_prefetch=2,
            grid=(1,),
            in_specs=[whole(k.shape), whole(v.shape)],
            out_specs=[whole(shape), whole(shape)],
        ),
        out_shape=[jax.ShapeDtypeStruct(shape, BF16)] * 2,
        compiler_params=pltpu.CompilerParams(vmem_limit_bytes=12 * MIB),
        cost_estimate=pl.CostEstimate(
            flops=1_000_000_000, bytes_accessed=1_000_000, transcendentals=0
        ),
        name="pack_video",
    )(first, lengths, k, v)


def video_kernel(
    first_ref,
    pairs_ref,
    len_ref,
    q_ref,
    do_ref,
    before_ref,
    own_ref,
    after_ref,
    out_ref,
    dq_ref,
    gbefore_ref,
    gown_ref,
    gafter_ref,
    kc,
    vc,
    bias,
    dk_acc,
    dv_acc,
    kbd,
    vbd,
    s_scr,
    p_scr,
    offsets,
):
    j = pl.program_id(0)
    first = first_ref[0]
    sources = (
        (before_ref, gbefore_ref, 0, REACH),
        (own_ref, gown_ref, REACH, SPAN),
        (after_ref, gafter_ref, REACH + SPAN, REACH),
    )
    row = block_row(BA, WIDE)
    narrow_row = block_row(BA, BA)

    @pl.when(j == 0)
    def _():
        for i in range(P_SIZE):
            clear_corners(kbd.at[i])
            clear_corners(vbd.at[i])

        def clear(i, carry):
            rows = pl.ds(i * BA, BA)
            kc[rows, :] = jnp.zeros((BA, WIDE), BF16)
            vc[rows, :] = jnp.zeros((BA, WIDE), BF16)
            bias[rows, :] = jnp.full((BA, BA), NEG, F32)
            dk_acc[rows, :] = jnp.zeros((BA, WIDE), F32)
            dv_acc[rows, :] = jnp.zeros((BA, WIDE), F32)
            return carry

        lax.fori_loop(0, EXT + 1, clear, 0)
        offset = jnp.int32(0)
        for source, _, base, count in sources:

            def one(i, offset, source=source, base=base):
                length = len_ref[global_block(first, base + i)]
                rows = pl.ds(aligned(offset), BA)
                offsets[base + i] = offset
                kc[rows, :] = pick(row < length, source[i, 0], jnp.zeros((BA, WIDE), BF16))
                vc[rows, :] = pick(row < length, source[i, 1], jnp.zeros((BA, WIDE), BF16))
                bias[rows, :] = pick(narrow_row < length, 0.0, NEG)
                return offset + padded(length)

            offset = lax.fori_loop(0, count, one, offset)
        offsets[EXT] = offset

    start = pairs_ref[first + j, 0]
    e = start - first + REACH
    low = offsets[e]
    high = offsets[e + P_SIZE]
    groups = (high - low + BA - 1) // BA
    place = lax.broadcasted_iota(jnp.int32, (BA, BA), 1)

    def attend(count):
        q = q_ref[...]
        do = do_ref[...]
        spots = []
        for i in range(count):
            begin = jnp.minimum(low + i * BA, AUDIO_ROWS)
            rows = pl.ds(aligned(begin), BA)
            spots.append(rows)
            put_diagonal(kbd.at[i], kc[rows, :])
            put_diagonal(vbd.at[i], vc[rows, :])
        top = None
        for i in range(count):
            begin = jnp.minimum(low + i * BA, AUDIO_ROWS)
            shut = pick(place < high - begin, bias[spots[i], :].T, NEG)[0:1, :]
            s = dot_nt(q, kbd[i]) + jnp.concatenate([shut, shut], axis=1)
            s_scr[i] = s
            top = s if top is None else jnp.maximum(top, s)
        peak = C2 * split_rows(
            jnp.max(top[:, 0:DH], axis=1, keepdims=True),
            jnp.max(top[:, DH:WIDE], axis=1, keepdims=True),
            BV,
        )
        total = None
        acc = None
        for i in range(count):
            ex = jnp.exp2(s_scr[i] * C2 - peak)
            total = ex if total is None else total + ex
            p = ex.astype(BF16)
            p_scr[i] = p
            part = dot_nn(p, vbd[i])
            acc = part if acc is None else acc + part
        scale = 1.0 / split_rows(
            jnp.sum(total[:, 0:DH], axis=1, keepdims=True),
            jnp.sum(total[:, DH:WIDE], axis=1, keepdims=True),
            BV,
        )
        out = acc * scale
        out_ref[...] = out.astype(BF16)
        do_wide = do.astype(F32)
        prod = do_wide * out
        delta = split_rows(
            jnp.sum(prod[:, 0:DH], axis=1, keepdims=True),
            jnp.sum(prod[:, DH:WIDE], axis=1, keepdims=True),
            BV,
        )
        scale_in = scale * INV_ROOT
        q_t = (q.astype(F32) * scale_in).astype(BF16).T
        do_t = (do_wide * scale).astype(BF16).T
        acc = None
        for i in range(count):
            dp = dot_nt(do, vbd[i])
            p = p_scr[i]
            ds = (p.astype(F32) * (dp - delta)).astype(BF16)
            part = dot_nn(ds, kbd[i])
            acc = part if acc is None else acc + part
            for h in range(2):
                cut = slice(h * DH, (h + 1) * DH)
                dk_acc[spots[i], cut] += dot_nn(q_t[cut, :], ds[:, cut]).T
                dv_acc[spots[i], cut] += dot_nn(do_t[cut, :], p[:, cut]).T
        dq_ref[...] = (acc * scale_in).astype(BF16)

    below = 0
    for count in GROUP_FORMS:
        pl.when(jnp.logical_and(groups > below, groups <= count))(functools.partial(attend, count))
        below = count

    @pl.when(j == pl.num_programs(0) - 1)
    def _():
        for _, target, base, count in sources:

            def one(i, carry, target=target, base=base):
                length = len_ref[global_block(first, base + i)]
                rows = pl.ds(aligned(offsets[base + i]), BA)
                target[i, 0] = pick(row < length, dk_acc[rows, :], 0.0).astype(target.dtype)
                target[i, 1] = pick(row < length, dv_acc[rows, :], 0.0).astype(target.dtype)
                return carry

            lax.fori_loop(0, count, one, 0)


def whole(shape):
    return pl.BlockSpec(shape, lambda *_: (0,) * len(shape), pipeline_mode=pl.Buffered(1))


def run_video(first, pairs, lengths, q, do, before, own, after):
    rows = pl.BlockSpec((BV, WIDE), lambda j, *_: (j, 0))
    return pl.pallas_call(
        video_kernel,
        grid_spec=pltpu.PrefetchScalarGridSpec(
            num_scalar_prefetch=3,
            grid=(SPAN,),
            in_specs=[rows, rows, whole(before.shape), whole(own.shape), whole(after.shape)],
            out_specs=[rows, rows, whole(before.shape), whole(own.shape), whole(after.shape)],
            scratch_shapes=[
                pltpu.VMEM((AUDIO_ROWS + BA, WIDE), BF16),
                pltpu.VMEM((AUDIO_ROWS + BA, WIDE), BF16),
                pltpu.VMEM((AUDIO_ROWS + BA, BA), F32),
                pltpu.VMEM((AUDIO_ROWS + BA, WIDE), F32),
                pltpu.VMEM((AUDIO_ROWS + BA, WIDE), F32),
                pltpu.VMEM((P_SIZE, WIDE, WIDE), BF16),
                pltpu.VMEM((P_SIZE, WIDE, WIDE), BF16),
                pltpu.VMEM((P_SIZE, BV, WIDE), F32),
                pltpu.VMEM((P_SIZE, BV, WIDE), BF16),
                pltpu.SMEM((32,), jnp.int32),
            ],
        ),
        out_shape=[
            jax.ShapeDtypeStruct(q.shape, BF16),
            jax.ShapeDtypeStruct(q.shape, BF16),
            jax.ShapeDtypeStruct(before.shape, BF16),
            jax.ShapeDtypeStruct(own.shape, F32),
            jax.ShapeDtypeStruct(after.shape, BF16),
        ],
        compiler_params=pltpu.CompilerParams(vmem_limit_bytes=32 * MIB),
        cost_estimate=pl.CostEstimate(
            flops=20_000_000_000, bytes_accessed=20_000_000, transcendentals=0
        ),
        name="video_queries",
    )(first, pairs, lengths, q, do, before, own, after)


def packed_range(first, pairs_ref, offsets, block):
    inside = jnp.logical_and(block >= 0, block < NB)
    start = pairs_ref[jnp.clip(block, 0, NB - 1), 0] - first
    low = offsets[jnp.clip(start, 0, SPAN)]
    high = offsets[jnp.clip(start + P_SIZE, 0, SPAN)]
    return low, pick(inside, high, low)


def fill_bias(first, len_ref, bias, offsets):
    row = block_row(BV, BA)

    def one(c, offset):
        length = len_ref[first + c]
        offsets[c] = offset
        bias[pl.ds(aligned(offset), BV), :] = pick(row < length, 0.0, NEG)
        return offset + padded(length)

    end = lax.fori_loop(0, SPAN, one, 0)
    offsets[SPAN] = end
    bias[pl.ds(aligned(end), BV), :] = jnp.full((BV, BA), NEG, F32)


def part_kernel(pieces, letters, first_ref, pairs_ref, len_ref, *refs):
    n = len(pieces)
    sources = refs[:n]
    rest = refs[n:]
    if letters:
        own_st_ref = rest[0]
        rest = rest[1:]
    kc_ref, vc_ref = rest[:2]
    targets = rest[2 : 2 + n]
    st_ref, qbd, o_scr, s_scr, bias, offsets = rest[2 + n :]
    b = pl.program_id(0)
    first = first_ref[0]

    @pl.when(b == 0)
    def _():
        clear_corners(qbd)
        fill_bias(first, len_ref, bias, offsets)

    block = first
    for base, begin, count in pieces:
        inside = jnp.logical_and(b >= begin, b < begin + count)
        block = pick(inside, first + base + b - begin, block)
    low, high = packed_range(first, pairs_ref, offsets, block)
    chunks = (high - low + BV - 1) // BV
    row = block_row(BV, BA)

    @pl.when(chunks == 0)
    def _():
        o_scr[...] = jnp.zeros((WIDE, BA), F32)
        st_ref[0, 0:1, :] = jnp.full((1, WIDE), NEG, F32)
        st_ref[0, 1:2, :] = jnp.zeros((1, WIDE), F32)

    for (_, begin, count), source in zip(pieces, sources):

        @pl.when(jnp.logical_and(chunks > 0, jnp.logical_and(b >= begin, b < begin + count)))
        def _(source=source, begin=begin):
            put_diagonal(qbd, source[b - begin, 0])

    def attend(count):
        spots = [aligned(low + i * BV) for i in range(count)]
        peak = None
        for i, spot in enumerate(spots):
            rows = pl.ds(spot, BV)
            shut = bias[rows, :]
            if i == count - 1:
                shut = pick(row < high - spot, shut, NEG)
            s = dot_nt(kc_ref[rows, :], qbd[...]) + jnp.concatenate([shut, shut], axis=1)
            s_scr[i] = s
            top = jnp.max(s, axis=0, keepdims=True)
            peak = top if peak is None else jnp.maximum(peak, top)
        peak = peak * C2
        total = None
        acc = [None, None]
        for i, spot in enumerate(spots):
            ex = jnp.exp2(s_scr[i] * C2 - peak)
            part = jnp.sum(ex, axis=0, keepdims=True)
            total = part if total is None else total + part
            p = ex.astype(BF16)
            v_t = vc_ref[pl.ds(spot, BV), :].T
            for h in range(2):
                cut = slice(h * DH, (h + 1) * DH)
                part = dot_nn(v_t[cut, :], p[:, cut])
                acc[h] = part if acc[h] is None else acc[h] + part
        scale = 1.0 / total
        st_ref[0, 0:1, :] = peak + jnp.log2(total)
        for h in range(2):
            cut = slice(h * DH, (h + 1) * DH)
            o_scr[cut, :] = acc[h] * scale[:, cut]

    for count in range(1, SPAN + 1):
        pl.when(chunks == count)(functools.partial(attend, count))

    for n, ((_, begin, count), source, target) in enumerate(zip(pieces, sources, targets)):

        @pl.when(jnp.logical_and(b >= begin, b < begin + count))
        def _(n=n, source=source, target=target, begin=begin):
            for h in range(2):
                cut = slice(h * DH, (h + 1) * DH)
                do_t = source[b - begin, 1, :, cut].T.astype(F32)
                st_ref[0, 1:2, cut] = jnp.sum(o_scr[cut, :] * do_t, axis=0, keepdims=True)
            target[b - begin, 0:WIDE, :] = o_scr[...].astype(target.dtype)
            if letters:
                write_note(target, b - begin, WIDE, (st_ref[0, 0:1, :], st_ref[0, 1:2, :]))
                mine = own_st_ref[b - begin + n]
                write_note(target, b - begin, WIDE + NOTE, (mine[0:1, :], mine[1:2, :]))


def run_part(pieces, first, pairs, lengths, sources, kc, vc, own_stats=None):
    count = sum(piece[2] for piece in pieces)
    letters = own_stats is not None
    operands = (*sources, own_stats, kc, vc) if letters else (*sources, kc, vc)
    targets = [(piece[2], LETTER if letters else WIDE, BA) for piece in pieces]
    return pl.pallas_call(
        functools.partial(part_kernel, pieces, letters),
        grid_spec=pltpu.PrefetchScalarGridSpec(
            num_scalar_prefetch=3,
            grid=(count,),
            in_specs=[whole(a.shape) for a in operands],
            out_specs=[whole(x) for x in targets]
            + [pl.BlockSpec((1, 8, WIDE), lambda b, *_: (b, 0, 0))],
            scratch_shapes=[
                pltpu.VMEM((WIDE, WIDE), BF16),
                pltpu.VMEM((WIDE, BA), F32),
                pltpu.VMEM((SPAN, BV, WIDE), F32),
                pltpu.VMEM((VIDEO_ROWS + BV, BA), F32),
                pltpu.SMEM((16,), jnp.int32),
            ],
        ),
        out_shape=[jax.ShapeDtypeStruct(x, BF16 if letters else F32) for x in targets]
        + [jax.ShapeDtypeStruct((count, 8, WIDE), F32)],
        compiler_params=pltpu.CompilerParams(vmem_limit_bytes=20 * MIB),
        cost_estimate=pl.CostEstimate(
            flops=1_000_000_000, bytes_accessed=1_000_000, transcendentals=0
        ),
        name="audio_parts",
    )(first, pairs, lengths, *operands)


def grad_kernel(
    first_ref,
    pairs_ref,
    len_ref,
    before_ref,
    after_ref,
    own_ref,
    st_near_ref,
    st_own_ref,
    above_ref,
    below_ref,
    o_ref,
    kc_ref,
    vc_ref,
    dqb_ref,
    dqa_ref,
    dqo_ref,
    out_ref,
    dk_ref,
    dv_ref,
    qbd,
    dobd,
    acc,
    bias,
    offsets,
    st_scr,
    dk_acc,
    dv_acc,
):
    sources = (before_ref, after_ref, own_ref)
    targets = (dqb_ref, dqa_ref, dqo_ref)
    pieces = HALO + ((0, 2 * REACH, SPAN),)
    b = pl.program_id(0)
    first = first_ref[0]

    @pl.when(b == 0)
    def _():
        clear_corners(qbd)
        clear_corners(dobd)
        fill_bias(first, len_ref, bias, offsets)

        def clear(c, carry):
            rows = pl.ds(pl.multiple_of(c * BV, BV), BV)
            dk_acc[rows, :] = jnp.zeros((BV, WIDE), F32)
            dv_acc[rows, :] = jnp.zeros((BV, WIDE), F32)
            return carry

        lax.fori_loop(0, SPAN + 1, clear, 0)

    block = first
    for base, begin, count in pieces:
        inside = jnp.logical_and(b >= begin, b < begin + count)
        block = pick(inside, first + base + b - begin, block)
    low, high = packed_range(first, pairs_ref, offsets, block)
    chunks = (high - low + BV - 1) // BV
    row = block_row(BV, BA)
    for (_, begin, count), source, target in zip(pieces, sources, targets):
        inside = jnp.logical_and(b >= begin, b < begin + count)

        @pl.when(jnp.logical_and(chunks > 0, inside))
        def _(source=source, begin=begin):
            put_diagonal(qbd, source[b - begin, 0])
            put_diagonal(dobd, source[b - begin, 1])

        @pl.when(jnp.logical_and(chunks == 0, inside))
        def _(target=target, begin=begin):
            target[b - begin] = jnp.zeros((BA, WIDE), target.dtype)

    @pl.when(b < 2 * REACH)
    def _():
        mine = st_near_ref[jnp.minimum(b, 2 * REACH - 1)]
        is_before = b < REACH
        slot = jnp.clip(pick(is_before, b, b - REACH), 0, REACH - 1)
        below = read_note(below_ref, slot, WIDE + NOTE)
        above = read_note(above_ref, slot, WIDE + NOTE)
        other = [pick(is_before, x, y) for x, y in zip(below, above)]
        top = jnp.maximum(mine[0:1], other[0])
        log_total = top + jnp.log2(jnp.exp2(mine[0:1] - top) + jnp.exp2(other[0] - top))
        st_scr[0:1, :] = log_total
        st_scr[1:2, :] = (
            jnp.exp2(mine[0:1] - log_total) * mine[1:2] + jnp.exp2(other[0] - log_total) * other[1]
        )

    @pl.when(b >= 2 * REACH)
    def _():
        slot = b - 2 * REACH
        mine = st_own_ref[slot]
        up_slot = jnp.maximum(slot - 1, 0)
        down_slot = jnp.minimum(slot, REACH - 1)
        above = read_note(above_ref, up_slot, WIDE)
        below = read_note(below_ref, down_slot, WIDE)
        logs = [
            mine[0:1],
            pick(slot >= 1, above[0], NEG),
            pick(slot < REACH, below[0], NEG),
        ]
        parts = [mine[1:2], above[1], below[1]]
        top = functools.reduce(jnp.maximum, logs)
        log_total = top + jnp.log2(sum(jnp.exp2(x - top) for x in logs))
        shares = [jnp.exp2(x - log_total) for x in logs]
        st_scr[0:1, :] = log_total
        st_scr[1:2, :] = sum(x * y for x, y in zip(shares, parts))
        for h in range(2):
            cut = slice(h * DH, (h + 1) * DH)
            whole_out = (
                o_ref[slot, cut, :] * shares[0][:, cut]
                + above_ref[up_slot, cut, :].astype(F32) * shares[1][:, cut]
                + below_ref[down_slot, cut, :].astype(F32) * shares[2][:, cut]
            )
            out_ref[slot, :, cut] = whole_out.T.astype(BF16)

    log_total = st_scr[0:1, :]
    delta = st_scr[1:2, :]

    @pl.when(chunks > 0)
    def _():
        acc[...] = jnp.zeros((WIDE, BA), F32)

    def step(i, carry):
        begin = aligned(low + i * BV)
        rows = pl.ds(begin, BV)
        shut = pick(row < high - begin, bias[rows, :], NEG)
        k = kc_ref[rows, :]
        s = dot_nt(k, qbd[...])
        w = jnp.exp2(s * C2 - log_total + jnp.concatenate([shut, shut], axis=1))
        dp = dot_nt(vc_ref[rows, :], dobd[...])
        ds = (w * (dp - delta)).astype(BF16)
        w = w.astype(BF16)
        dv_acc[rows, :] += dot_nn(w, dobd[...])
        dk_acc[rows, :] += dot_nn(ds, qbd[...])
        k_t = k.T
        for h in range(2):
            cut = slice(h * DH, (h + 1) * DH)
            acc[cut, :] += dot_nn(k_t[cut, :], ds[:, cut])
        return carry

    lax.fori_loop(0, chunks, step, 0)
    for (_, begin, count), target in zip(pieces, targets):

        @pl.when(jnp.logical_and(chunks > 0, jnp.logical_and(b >= begin, b < begin + count)))
        def _(target=target, begin=begin):
            for h in range(2):
                cut = slice(h * DH, (h + 1) * DH)
                target[b - begin, :, cut] = (acc[cut, :].T * INV_ROOT).astype(target.dtype)

    @pl.when(b == pl.num_programs(0) - 1)
    def _():
        full_row = block_row(BV, WIDE)

        def drain(c, offset):
            length = len_ref[first + c]
            rows = pl.ds(aligned(offset), BV)
            valid = full_row < length
            dk_ref[c] = (pick(valid, dk_acc[rows, :], 0.0) * INV_ROOT).astype(BF16)
            dv_ref[c] = pick(valid, dv_acc[rows, :], 0.0).astype(BF16)
            return offset + padded(length)

        lax.fori_loop(0, SPAN, drain, 0)


def run_grad(first, pairs, lengths, near, own, st_near, st_own, above, below, o_t, kc, vc):
    operands = (*near, own, st_near, st_own, above, below, o_t, kc, vc)
    narrow = jax.ShapeDtypeStruct((REACH, BA, WIDE), BF16)
    outs = [
        narrow,
        narrow,
        jax.ShapeDtypeStruct((SPAN, BA, WIDE), F32),
        jax.ShapeDtypeStruct((SPAN, BA, WIDE), BF16),
        jax.ShapeDtypeStruct((SPAN, BV, WIDE), BF16),
        jax.ShapeDtypeStruct((SPAN, BV, WIDE), BF16),
    ]
    return pl.pallas_call(
        grad_kernel,
        grid_spec=pltpu.PrefetchScalarGridSpec(
            num_scalar_prefetch=3,
            grid=(EXT,),
            in_specs=[whole(a.shape) for a in operands],
            out_specs=[whole(x.shape) for x in outs],
            scratch_shapes=[
                pltpu.VMEM((WIDE, WIDE), BF16),
                pltpu.VMEM((WIDE, WIDE), BF16),
                pltpu.VMEM((WIDE, BA), F32),
                pltpu.VMEM((VIDEO_ROWS + BV, BA), F32),
                pltpu.SMEM((16,), jnp.int32),
                pltpu.VMEM((8, WIDE), F32),
                pltpu.VMEM((VIDEO_ROWS + BV, WIDE), F32),
                pltpu.VMEM((VIDEO_ROWS + BV, WIDE), F32),
            ],
        ),
        out_shape=outs,
        compiler_params=pltpu.CompilerParams(vmem_limit_bytes=32 * MIB),
        cost_estimate=pl.CostEstimate(
            flops=1_000_000_000, bytes_accessed=1_000_000, transcendentals=0
        ),
        name="audio_gradients",
    )(first, pairs, lengths, *operands)


def routes(ring):
    size = lax.axis_size("vid")
    count = size if ring else size - 1
    up = [(i, (i + 1) % size) for i in range(count)]
    return up, [(j, i) for i, j in up]


def span_tiles(*arrays):
    tiles = jnp.stack([a.reshape(BA, 8, WIDE) for a in arrays], axis=1)
    return jnp.transpose(tiles, (2, 1, 0, 3))


def to_span(tiles):
    return lax.all_to_all(tiles, "aud", split_axis=0, concat_axis=0, tiled=True)


def to_owner(tiles):
    return lax.all_to_all(tiles, "aud", split_axis=0, concat_axis=0, tiled=True)


def side_by_side(back):
    return [
        jnp.transpose(back[:, i], (1, 0, 2)).reshape(BA, 8 * WIDE) for i in range(back.shape[1])
    ]


def halo(tiles):
    up, down = routes(False)
    return lax.ppermute(tiles[1:], "vid", up), lax.ppermute(tiles[:-1], "vid", down)


def give_back(before, after):
    up, down = routes(False)
    return lax.ppermute(before, "vid", down), lax.ppermute(after, "vid", up)


def spread_low(part):
    return jnp.pad(part, ((0, 1),) + ((0, 0),) * (part.ndim - 1))


def spread_high(part):
    return jnp.pad(part, ((1, 0),) + ((0, 0),) * (part.ndim - 1))


def per_device(
    video_q,
    video_k,
    video_v,
    video_dout,
    audio_q,
    audio_k,
    audio_v,
    audio_dout,
    video_pairs,
    audio_pairs,
    video_len,
    audio_len,
):
    first = (lax.axis_index("vid") * SPAN).astype(jnp.int32).reshape(1)
    k = video_k.reshape(SPAN, BV, WIDE)
    v = video_v.reshape(SPAN, BV, WIDE)
    kc, vc = run_pack(first, video_len, k, v)
    qd = to_span(span_tiles(audio_q, audio_dout))
    kv_tiles = span_tiles(audio_k, audio_v)
    kv_tiles, kc, vc = lax.optimization_barrier((kv_tiles, kc, vc))
    qd_before, qd_after = halo(qd)
    kv = to_span(kv_tiles)
    o_own, st_own = run_part(OWN, first, audio_pairs, video_len, (qd,), kc, vc)
    kv_before, kv_after = halo(kv)

    near = (qd_before, qd_after)
    to_below, to_above, st_near = run_part(
        HALO, first, audio_pairs, video_len, near, kc, vc, st_own
    )
    st_near, audio_len = lax.optimization_barrier((st_near, audio_len))
    up, down = routes(True)
    above = lax.ppermute(to_below, "vid", down)
    below = lax.ppermute(to_above, "vid", up)

    video_out, video_dq, g_before, g_own, g_after = run_video(
        first, video_pairs, audio_len, video_q, video_dout, kv_before, kv, kv_after
    )
    g_before, g_after, above, below, later_len = lax.optimization_barrier(
        (g_before, g_after, above, below, video_len)
    )
    g_above, g_below = give_back(g_before, g_after)

    dq_before, dq_after, dq_own, out, video_dk, video_dv = run_grad(
        first, audio_pairs, later_len, near, qd, st_near, st_own, above, below, o_own, kc, vc
    )
    dq_above, dq_below = give_back(dq_before, dq_after)

    g = (g_own + spread_high(g_above).astype(F32) + spread_low(g_below).astype(F32)).astype(BF16)
    g, dq_own = lax.optimization_barrier((g, dq_own))
    g_back = to_owner(g)
    dq = (dq_own + spread_high(dq_above).astype(F32) + spread_low(dq_below).astype(F32)).astype(BF16)
    od, g_back = lax.optimization_barrier((jnp.stack([out, dq], axis=1), g_back))
    audio_dk, audio_dv = side_by_side(g_back)
    audio_out, audio_dq = side_by_side(to_owner(od))
    return (
        video_out,
        audio_out,
        video_dq,
        video_dk.reshape(video_k.shape),
        video_dv.reshape(video_k.shape),
        audio_dq,
        audio_dk,
        audio_dv,
    )


def solution(mesh):
    video = P("vid", "aud")
    audio = P(("vid", "aud"), None)
    return jax.shard_map(
        per_device,
        mesh=mesh,
        in_specs=(video,) * 4 + (audio,) * 4 + (P(),) * 4,
        out_specs=(video, audio, video, video, video, audio, audio, audio),
        check_vma=False,
    )
```

```python
import functools
import math

import jax
import jax.numpy as jnp
from jax import lax
from jax.experimental import pallas as pl
from jax.experimental.pallas import tpu as pltpu
from jax.sharding import PartitionSpec as P

DH = 128
BV = 512
BA = 128
P_SIZE = 8
NB = 128
SPAN = 8
REACH = P_SIZE - 1
EXT = SPAN + 2 * REACH
WIDE = 2 * DH
NEG = -1e30
INV_ROOT = 1.0 / math.sqrt(DH)
C2 = math.log2(math.e) / math.sqrt(DH)
F32 = jnp.float32
BF16 = jnp.bfloat16
MIB = 1024 * 1024
PACK = 16
OWN = ((0, 0, SPAN),)
HALO = ((-REACH, 0, REACH), (SPAN, REACH, REACH))
GROUP_FORMS = (4, 5, 6, 7, 8)
VIDEO_ROWS = SPAN * BV
AUDIO_ROWS = EXT * BA
NOTE = 16
LETTER = WIDE + 2 * NOTE


def dot_nt(a, b):
    return lax.dot_general(a, b, (((1,), (1,)), ((), ())), preferred_element_type=F32)


def dot_nn(a, b):
    return jnp.dot(a, b, preferred_element_type=F32)


def split_rows(column0, column1, rows):
    return jnp.concatenate(
        [jnp.broadcast_to(column0, (rows, DH)), jnp.broadcast_to(column1, (rows, DH))], axis=1
    )


def put_diagonal(ref, tile):
    ref[0:DH, 0:DH] = tile[:, 0:DH]
    ref[DH:WIDE, DH:WIDE] = tile[:, DH:WIDE]


def clear_corners(ref):
    ref[0:DH, DH:WIDE] = jnp.zeros((DH, DH), ref.dtype)
    ref[DH:WIDE, 0:DH] = jnp.zeros((DH, DH), ref.dtype)


def write_note(ref, i, row, stats):
    lines = []
    for stat in stats:
        for h in range(2):
            rest = stat[:, h * DH : (h + 1) * DH]
            for _ in range(3):
                piece = rest.astype(BF16)
                rest = rest - piece.astype(F32)
                lines.append(piece.astype(F32))
    lines.append(jnp.zeros((NOTE - len(lines), DH), F32))
    ref[i, row : row + NOTE, :] = jnp.concatenate(lines, axis=0).astype(BF16)


def read_note(ref, i, row):
    note = ref[i, row : row + NOTE, :].astype(F32)
    wide = []
    for k in range(4):
        wide.append(note[3 * k : 3 * k + 1] + note[3 * k + 1 : 3 * k + 2] + note[3 * k + 2 : 3 * k + 3])
    return (
        jnp.concatenate(wide[0:2], axis=1),
        jnp.concatenate(wide[2:4], axis=1),
    )


def padded(length):
    return (length + PACK - 1) // PACK * PACK


def aligned(row):
    return pl.multiple_of(row, PACK)


def pick(cond, value, other):
    return jnp.where(cond, value, other)


def block_row(count, width):
    return lax.broadcasted_iota(jnp.int32, (count, width), 0)


def global_block(first, e):
    return jnp.clip(first - REACH + e, 0, NB - 1)


def pack_kernel(first_ref, len_ref, k_ref, v_ref, kc_ref, vc_ref):
    first = first_ref[0]
    row = block_row(BV, WIDE)
    zeros = jnp.zeros((BV, WIDE), BF16)

    def one(c, offset):
        length = len_ref[first + c]
        rows = pl.ds(aligned(offset), BV)
        kc_ref[rows, :] = pick(row < length, k_ref[c], zeros)
        vc_ref[rows, :] = pick(row < length, v_ref[c], zeros)
        return offset + padded(length)

    end = lax.fori_loop(0, SPAN, one, 0)
    rows = pl.ds(aligned(end), BV)
    kc_ref[rows, :] = zeros
    vc_ref[rows, :] = zeros


def run_pack(first, lengths, k, v):
    shape = (VIDEO_ROWS + BV, WIDE)
    return pl.pallas_call(
        pack_kernel,
        grid_spec=pltpu.PrefetchScalarGridSpec(
            num_scalar_prefetch=2,
            grid=(1,),
            in_specs=[whole(k.shape), whole(v.shape)],
            out_specs=[whole(shape), whole(shape)],
        ),
        out_shape=[jax.ShapeDtypeStruct(shape, BF16)] * 2,
        compiler_params=pltpu.CompilerParams(vmem_limit_bytes=12 * MIB),
        cost_estimate=pl.CostEstimate(
            flops=1_000_000_000, bytes_accessed=1_000_000, transcendentals=0
        ),
        name="pack_video",
    )(first, lengths, k, v)


def video_kernel(
    first_ref,
    pairs_ref,
    len_ref,
    q_ref,
    do_ref,
    before_ref,
    own_ref,
    after_ref,
    out_ref,
    dq_ref,
    gbefore_ref,
    gown_ref,
    gafter_ref,
    kc,
    vc,
    bias,
    dk_acc,
    dv_acc,
    kbd,
    vbd,
    s_scr,
    p_scr,
    offsets,
):
    j = pl.program_id(0)
    first = first_ref[0]
    sources = (
        (before_ref, gbefore_ref, 0, REACH),
        (own_ref, gown_ref, REACH, SPAN),
        (after_ref, gafter_ref, REACH + SPAN, REACH),
    )
    row = block_row(BA, WIDE)
    narrow_row = block_row(BA, BA)

    @pl.when(j == 0)
    def _():
        for i in range(P_SIZE):
            clear_corners(kbd.at[i])
            clear_corners(vbd.at[i])

        def clear(i, carry):
            rows = pl.ds(i * BA, BA)
            kc[rows, :] = jnp.zeros((BA, WIDE), BF16)
            vc[rows, :] = jnp.zeros((BA, WIDE), BF16)
            bias[rows, :] = jnp.full((BA, BA), NEG, F32)
            dk_acc[rows, :] = jnp.zeros((BA, WIDE), F32)
            dv_acc[rows, :] = jnp.zeros((BA, WIDE), F32)
            return carry

        lax.fori_loop(0, EXT + 1, clear, 0)
        offset = jnp.int32(0)
        for source, _, base, count in sources:

            def one(i, offset, source=source, base=base):
                length = len_ref[global_block(first, base + i)]
                rows = pl.ds(aligned(offset), BA)
                offsets[base + i] = offset
                kc[rows, :] = pick(row < length, source[i, 0], jnp.zeros((BA, WIDE), BF16))
                vc[rows, :] = pick(row < length, source[i, 1], jnp.zeros((BA, WIDE), BF16))
                bias[rows, :] = pick(narrow_row < length, 0.0, NEG)
                return offset + padded(length)

            offset = lax.fori_loop(0, count, one, offset)
        offsets[EXT] = offset

    start = pairs_ref[first + j, 0]
    e = start - first + REACH
    low = offsets[e]
    high = offsets[e + P_SIZE]
    groups = (high - low + BA - 1) // BA
    place = lax.broadcasted_iota(jnp.int32, (BA, BA), 1)

    def attend(count):
        q = q_ref[...]
        do = do_ref[...]
        spots = []
        for i in range(count):
            begin = jnp.minimum(low + i * BA, AUDIO_ROWS)
            rows = pl.ds(aligned(begin), BA)
            spots.append(rows)
            put_diagonal(kbd.at[i], kc[rows, :])
            put_diagonal(vbd.at[i], vc[rows, :])
        top = None
        for i in range(count):
            begin = jnp.minimum(low + i * BA, AUDIO_ROWS)
            shut = pick(place < high - begin, bias[spots[i], :].T, NEG)[0:1, :]
            s = dot_nt(q, kbd[i]) + jnp.concatenate([shut, shut], axis=1)
            s_scr[i] = s
            top = s if top is None else jnp.maximum(top, s)
        peak = C2 * split_rows(
            jnp.max(top[:, 0:DH], axis=1, keepdims=True),
            jnp.max(top[:, DH:WIDE], axis=1, keepdims=True),
            BV,
        )
        total = None
        acc = None
        for i in range(count):
            ex = jnp.exp2(s_scr[i] * C2 - peak)
            total = ex if total is None else total + ex
            p = ex.astype(BF16)
            p_scr[i] = p
            part = dot_nn(p, vbd[i])
            acc = part if acc is None else acc + part
        scale = 1.0 / split_rows(
            jnp.sum(total[:, 0:DH], axis=1, keepdims=True),
            jnp.sum(total[:, DH:WIDE], axis=1, keepdims=True),
            BV,
        )
        out = acc * scale
        out_ref[...] = out.astype(BF16)
        do_wide = do.astype(F32)
        prod = do_wide * out
        delta = split_rows(
            jnp.sum(prod[:, 0:DH], axis=1, keepdims=True),
            jnp.sum(prod[:, DH:WIDE], axis=1, keepdims=True),
            BV,
        )
        scale_in = scale * INV_ROOT
        q_t = (q.astype(F32) * scale_in).astype(BF16).T
        do_t = (do_wide * scale).astype(BF16).T
        acc = None
        for i in range(count):
            dp = dot_nt(do, vbd[i])
            p = p_scr[i]
            ds = (p.astype(F32) * (dp - delta)).astype(BF16)
            part = dot_nn(ds, kbd[i])
            acc = part if acc is None else acc + part
            for h in range(2):
                cut = slice(h * DH, (h + 1) * DH)
                dk_acc[spots[i], cut] += dot_nn(q_t[cut, :], ds[:, cut]).T
                dv_acc[spots[i], cut] += dot_nn(do_t[cut, :], p[:, cut]).T
        dq_ref[...] = (acc * scale_in).astype(BF16)

    below = 0
    for count in GROUP_FORMS:
        pl.when(jnp.logical_and(groups > below, groups <= count))(functools.partial(attend, count))
        below = count

    @pl.when(j == pl.num_programs(0) - 1)
    def _():
        for _, target, base, count in sources:

            def one(i, carry, target=target, base=base):
                length = len_ref[global_block(first, base + i)]
                rows = pl.ds(aligned(offsets[base + i]), BA)
                target[i, 0] = pick(row < length, dk_acc[rows, :], 0.0).astype(target.dtype)
                target[i, 1] = pick(row < length, dv_acc[rows, :], 0.0).astype(target.dtype)
                return carry

            lax.fori_loop(0, count, one, 0)


def whole(shape):
    return pl.BlockSpec(shape, lambda *_: (0,) * len(shape), pipeline_mode=pl.Buffered(1))


def run_video(first, pairs, lengths, q, do, before, own, after):
    rows = pl.BlockSpec((BV, WIDE), lambda j, *_: (j, 0))
    return pl.pallas_call(
        video_kernel,
        grid_spec=pltpu.PrefetchScalarGridSpec(
            num_scalar_prefetch=3,
            grid=(SPAN,),
            in_specs=[rows, rows, whole(before.shape), whole(own.shape), whole(after.shape)],
            out_specs=[rows, rows, whole(before.shape), whole(own.shape), whole(after.shape)],
            scratch_shapes=[
                pltpu.VMEM((AUDIO_ROWS + BA, WIDE), BF16),
                pltpu.VMEM((AUDIO_ROWS + BA, WIDE), BF16),
                pltpu.VMEM((AUDIO_ROWS + BA, BA), F32),
                pltpu.VMEM((AUDIO_ROWS + BA, WIDE), F32),
                pltpu.VMEM((AUDIO_ROWS + BA, WIDE), F32),
                pltpu.VMEM((P_SIZE, WIDE, WIDE), BF16),
                pltpu.VMEM((P_SIZE, WIDE, WIDE), BF16),
                pltpu.VMEM((P_SIZE, BV, WIDE), F32),
                pltpu.VMEM((P_SIZE, BV, WIDE), BF16),
                pltpu.SMEM((32,), jnp.int32),
            ],
        ),
        out_shape=[
            jax.ShapeDtypeStruct(q.shape, BF16),
            jax.ShapeDtypeStruct(q.shape, BF16),
            jax.ShapeDtypeStruct(before.shape, BF16),
            jax.ShapeDtypeStruct(own.shape, F32),
            jax.ShapeDtypeStruct(after.shape, BF16),
        ],
        compiler_params=pltpu.CompilerParams(vmem_limit_bytes=32 * MIB),
        cost_estimate=pl.CostEstimate(
            flops=20_000_000_000, bytes_accessed=20_000_000, transcendentals=0
        ),
        name="video_queries",
    )(first, pairs, lengths, q, do, before, own, after)


def packed_range(first, pairs_ref, offsets, block):
    inside = jnp.logical_and(block >= 0, block < NB)
    start = pairs_ref[jnp.clip(block, 0, NB - 1), 0] - first
    low = offsets[jnp.clip(start, 0, SPAN)]
    high = offsets[jnp.clip(start + P_SIZE, 0, SPAN)]
    return low, pick(inside, high, low)


def fill_bias(first, len_ref, bias, offsets):
    row = block_row(BV, BA)

    def one(c, offset):
        length = len_ref[first + c]
        offsets[c] = offset
        bias[pl.ds(aligned(offset), BV), :] = pick(row < length, 0.0, NEG)
        return offset + padded(length)

    end = lax.fori_loop(0, SPAN, one, 0)
    offsets[SPAN] = end
    bias[pl.ds(aligned(end), BV), :] = jnp.full((BV, BA), NEG, F32)


def part_kernel(pieces, letters, first_ref, pairs_ref, len_ref, *refs):
    n = len(pieces)
    sources = refs[:n]
    rest = refs[n:]
    if letters:
        own_st_ref = rest[0]
        rest = rest[1:]
    kc_ref, vc_ref = rest[:2]
    targets = rest[2 : 2 + n]
    st_ref, qbd, o_scr, s_scr, bias, offsets = rest[2 + n :]
    first = first_ref[0]
    clear_corners(qbd)
    fill_bias(first, len_ref, bias, offsets)

    def visit(b, carry):
        block = first
        for base, begin, count in pieces:
            inside = jnp.logical_and(b >= begin, b < begin + count)
            block = pick(inside, first + base + b - begin, block)
        low, high = packed_range(first, pairs_ref, offsets, block)
        chunks = (high - low + BV - 1) // BV
        row = block_row(BV, BA)

        @pl.when(chunks == 0)
        def _():
            o_scr[...] = jnp.zeros((WIDE, BA), F32)
            st_ref[b, 0:1, :] = jnp.full((1, WIDE), NEG, F32)
            st_ref[b, 1:2, :] = jnp.zeros((1, WIDE), F32)

        for (_, begin, count), source in zip(pieces, sources):

            @pl.when(jnp.logical_and(chunks > 0, jnp.logical_and(b >= begin, b < begin + count)))
            def _(source=source, begin=begin):
                put_diagonal(qbd, source[b - begin, 0])

        def attend(count):
            spots = [aligned(low + i * BV) for i in range(count)]
            peak = None
            for i, spot in enumerate(spots):
                rows = pl.ds(spot, BV)
                shut = bias[rows, :]
                if i == count - 1:
                    shut = pick(row < high - spot, shut, NEG)
                s = dot_nt(kc_ref[rows, :], qbd[...]) + jnp.concatenate([shut, shut], axis=1)
                s_scr[i] = s
                top = jnp.max(s, axis=0, keepdims=True)
                peak = top if peak is None else jnp.maximum(peak, top)
            peak = peak * C2
            total = None
            acc = [None, None]
            for i, spot in enumerate(spots):
                ex = jnp.exp2(s_scr[i] * C2 - peak)
                part = jnp.sum(ex, axis=0, keepdims=True)
                total = part if total is None else total + part
                p = ex.astype(BF16)
                v_t = vc_ref[pl.ds(spot, BV), :].T
                for h in range(2):
                    cut = slice(h * DH, (h + 1) * DH)
                    part = dot_nn(v_t[cut, :], p[:, cut])
                    acc[h] = part if acc[h] is None else acc[h] + part
            scale = 1.0 / total
            st_ref[b, 0:1, :] = peak + jnp.log2(total)
            for h in range(2):
                cut = slice(h * DH, (h + 1) * DH)
                o_scr[cut, :] = acc[h] * scale[:, cut]

        for count in range(1, SPAN + 1):
            pl.when(chunks == count)(functools.partial(attend, count))

        for n, ((_, begin, count), source, target) in enumerate(zip(pieces, sources, targets)):

            @pl.when(jnp.logical_and(b >= begin, b < begin + count))
            def _(n=n, source=source, target=target, begin=begin):
                for h in range(2):
                    cut = slice(h * DH, (h + 1) * DH)
                    do_t = source[b - begin, 1, :, cut].T.astype(F32)
                    st_ref[b, 1:2, cut] = jnp.sum(o_scr[cut, :] * do_t, axis=0, keepdims=True)
                target[b - begin, 0:WIDE, :] = o_scr[...].astype(target.dtype)
                if letters:
                    write_note(target, b - begin, WIDE, (st_ref[b, 0:1, :], st_ref[b, 1:2, :]))
                    mine = own_st_ref[b - begin + n]
                    write_note(target, b - begin, WIDE + NOTE, (mine[0:1, :], mine[1:2, :]))
        return carry

    lax.fori_loop(0, sum(piece[2] for piece in pieces), visit, 0)


def run_part(pieces, first, pairs, lengths, sources, kc, vc, own_stats=None):
    count = sum(piece[2] for piece in pieces)
    letters = own_stats is not None
    operands = (*sources, own_stats, kc, vc) if letters else (*sources, kc, vc)
    targets = [(piece[2], LETTER if letters else WIDE, BA) for piece in pieces]
    return pl.pallas_call(
        functools.partial(part_kernel, pieces, letters),
        grid_spec=pltpu.PrefetchScalarGridSpec(
            num_scalar_prefetch=3,
            grid=(1,),
            in_specs=[whole(a.shape) for a in operands],
            out_specs=[whole(x) for x in targets]
            + [whole((count, 8, WIDE))],
            scratch_shapes=[
                pltpu.VMEM((WIDE, WIDE), BF16),
                pltpu.VMEM((WIDE, BA), F32),
                pltpu.VMEM((SPAN, BV, WIDE), F32),
                pltpu.VMEM((VIDEO_ROWS + BV, BA), F32),
                pltpu.SMEM((16,), jnp.int32),
            ],
        ),
        out_shape=[jax.ShapeDtypeStruct(x, BF16 if letters else F32) for x in targets]
        + [jax.ShapeDtypeStruct((count, 8, WIDE), F32)],
        compiler_params=pltpu.CompilerParams(vmem_limit_bytes=20 * MIB),
        cost_estimate=pl.CostEstimate(
            flops=1_000_000_000, bytes_accessed=1_000_000, transcendentals=0
        ),
        name="audio_parts",
    )(first, pairs, lengths, *operands)


def grad_kernel(
    first_ref,
    pairs_ref,
    len_ref,
    before_ref,
    after_ref,
    own_ref,
    st_near_ref,
    st_own_ref,
    above_ref,
    below_ref,
    o_ref,
    kc_ref,
    vc_ref,
    dqb_ref,
    dqa_ref,
    dqo_ref,
    out_ref,
    dk_ref,
    dv_ref,
    qbd,
    dobd,
    acc,
    bias,
    offsets,
    st_scr,
    dk_acc,
    dv_acc,
):
    sources = (before_ref, after_ref, own_ref)
    targets = (dqb_ref, dqa_ref, dqo_ref)
    pieces = HALO + ((0, 2 * REACH, SPAN),)
    first = first_ref[0]
    clear_corners(qbd)
    clear_corners(dobd)
    fill_bias(first, len_ref, bias, offsets)

    def clear(c, carry):
        rows = pl.ds(pl.multiple_of(c * BV, BV), BV)
        dk_acc[rows, :] = jnp.zeros((BV, WIDE), F32)
        dv_acc[rows, :] = jnp.zeros((BV, WIDE), F32)
        return carry

    lax.fori_loop(0, SPAN + 1, clear, 0)

    def visit(b, carry):
        block = first
        for base, begin, count in pieces:
            inside = jnp.logical_and(b >= begin, b < begin + count)
            block = pick(inside, first + base + b - begin, block)
        low, high = packed_range(first, pairs_ref, offsets, block)
        chunks = (high - low + BV - 1) // BV
        row = block_row(BV, BA)
        for (_, begin, count), source, target in zip(pieces, sources, targets):
            inside = jnp.logical_and(b >= begin, b < begin + count)

            @pl.when(jnp.logical_and(chunks > 0, inside))
            def _(source=source, begin=begin):
                put_diagonal(qbd, source[b - begin, 0])
                put_diagonal(dobd, source[b - begin, 1])

            @pl.when(jnp.logical_and(chunks == 0, inside))
            def _(target=target, begin=begin):
                target[b - begin] = jnp.zeros((BA, WIDE), target.dtype)

        @pl.when(b < 2 * REACH)
        def _():
            mine = st_near_ref[jnp.minimum(b, 2 * REACH - 1)]
            is_before = b < REACH
            slot = jnp.clip(pick(is_before, b, b - REACH), 0, REACH - 1)
            below = read_note(below_ref, slot, WIDE + NOTE)
            above = read_note(above_ref, slot, WIDE + NOTE)
            other = [pick(is_before, x, y) for x, y in zip(below, above)]
            top = jnp.maximum(mine[0:1], other[0])
            log_total = top + jnp.log2(jnp.exp2(mine[0:1] - top) + jnp.exp2(other[0] - top))
            st_scr[0:1, :] = log_total
            st_scr[1:2, :] = (
                jnp.exp2(mine[0:1] - log_total) * mine[1:2] + jnp.exp2(other[0] - log_total) * other[1]
            )

        @pl.when(b >= 2 * REACH)
        def _():
            slot = b - 2 * REACH
            mine = st_own_ref[slot]
            up_slot = jnp.maximum(slot - 1, 0)
            down_slot = jnp.minimum(slot, REACH - 1)
            above = read_note(above_ref, up_slot, WIDE)
            below = read_note(below_ref, down_slot, WIDE)
            logs = [
                mine[0:1],
                pick(slot >= 1, above[0], NEG),
                pick(slot < REACH, below[0], NEG),
            ]
            parts = [mine[1:2], above[1], below[1]]
            top = functools.reduce(jnp.maximum, logs)
            log_total = top + jnp.log2(sum(jnp.exp2(x - top) for x in logs))
            shares = [jnp.exp2(x - log_total) for x in logs]
            st_scr[0:1, :] = log_total
            st_scr[1:2, :] = sum(x * y for x, y in zip(shares, parts))
            for h in range(2):
                cut = slice(h * DH, (h + 1) * DH)
                whole_out = (
                    o_ref[slot, cut, :] * shares[0][:, cut]
                    + above_ref[up_slot, cut, :].astype(F32) * shares[1][:, cut]
                    + below_ref[down_slot, cut, :].astype(F32) * shares[2][:, cut]
                )
                out_ref[slot, :, cut] = whole_out.T.astype(BF16)

        log_total = st_scr[0:1, :]
        delta = st_scr[1:2, :]

        @pl.when(chunks > 0)
        def _():
            acc[...] = jnp.zeros((WIDE, BA), F32)

        def step(i, carry):
            begin = aligned(low + i * BV)
            rows = pl.ds(begin, BV)
            shut = pick(row < high - begin, bias[rows, :], NEG)
            k = kc_ref[rows, :]
            s = dot_nt(k, qbd[...])
            w = jnp.exp2(s * C2 - log_total + jnp.concatenate([shut, shut], axis=1))
            dp = dot_nt(vc_ref[rows, :], dobd[...])
            ds = (w * (dp - delta)).astype(BF16)
            w = w.astype(BF16)
            dv_acc[rows, :] += dot_nn(w, dobd[...])
            dk_acc[rows, :] += dot_nn(ds, qbd[...])
            k_t = k.T
            for h in range(2):
                cut = slice(h * DH, (h + 1) * DH)
                acc[cut, :] += dot_nn(k_t[cut, :], ds[:, cut])
            return carry

        lax.fori_loop(0, chunks, step, 0)
        for (_, begin, count), target in zip(pieces, targets):

            @pl.when(jnp.logical_and(chunks > 0, jnp.logical_and(b >= begin, b < begin + count)))
            def _(target=target, begin=begin):
                for h in range(2):
                    cut = slice(h * DH, (h + 1) * DH)
                    target[b - begin, :, cut] = (acc[cut, :].T * INV_ROOT).astype(target.dtype)
        return carry

    lax.fori_loop(0, sum(piece[2] for piece in pieces), visit, 0)

    full_row = block_row(BV, WIDE)

    def drain(c, offset):
        length = len_ref[first + c]
        rows = pl.ds(aligned(offset), BV)
        valid = full_row < length
        dk_ref[c] = (pick(valid, dk_acc[rows, :], 0.0) * INV_ROOT).astype(BF16)
        dv_ref[c] = pick(valid, dv_acc[rows, :], 0.0).astype(BF16)
        return offset + padded(length)

    lax.fori_loop(0, SPAN, drain, 0)


def run_grad(first, pairs, lengths, near, own, st_near, st_own, above, below, o_t, kc, vc):
    operands = (*near, own, st_near, st_own, above, below, o_t, kc, vc)
    narrow = jax.ShapeDtypeStruct((REACH, BA, WIDE), BF16)
    outs = [
        narrow,
        narrow,
        jax.ShapeDtypeStruct((SPAN, BA, WIDE), F32),
        jax.ShapeDtypeStruct((SPAN, BA, WIDE), BF16),
        jax.ShapeDtypeStruct((SPAN, BV, WIDE), BF16),
        jax.ShapeDtypeStruct((SPAN, BV, WIDE), BF16),
    ]
    return pl.pallas_call(
        grad_kernel,
        grid_spec=pltpu.PrefetchScalarGridSpec(
            num_scalar_prefetch=3,
            grid=(1,),
            in_specs=[whole(a.shape) for a in operands],
            out_specs=[whole(x.shape) for x in outs],
            scratch_shapes=[
                pltpu.VMEM((WIDE, WIDE), BF16),
                pltpu.VMEM((WIDE, WIDE), BF16),
                pltpu.VMEM((WIDE, BA), F32),
                pltpu.VMEM((VIDEO_ROWS + BV, BA), F32),
                pltpu.SMEM((16,), jnp.int32),
                pltpu.VMEM((8, WIDE), F32),
                pltpu.VMEM((VIDEO_ROWS + BV, WIDE), F32),
                pltpu.VMEM((VIDEO_ROWS + BV, WIDE), F32),
            ],
        ),
        out_shape=outs,
        compiler_params=pltpu.CompilerParams(vmem_limit_bytes=32 * MIB),
        cost_estimate=pl.CostEstimate(
            flops=1_000_000_000, bytes_accessed=1_000_000, transcendentals=0
        ),
        name="audio_gradients",
    )(first, pairs, lengths, *operands)


def routes(ring):
    size = lax.axis_size("vid")
    count = size if ring else size - 1
    up = [(i, (i + 1) % size) for i in range(count)]
    return up, [(j, i) for i, j in up]


def span_tiles(*arrays):
    tiles = jnp.stack([a.reshape(BA, 8, WIDE) for a in arrays], axis=1)
    return jnp.transpose(tiles, (2, 1, 0, 3))


def to_span(tiles):
    return lax.all_to_all(tiles, "aud", split_axis=0, concat_axis=0, tiled=True)


def to_owner(tiles):
    return lax.all_to_all(tiles, "aud", split_axis=0, concat_axis=0, tiled=True)


def side_by_side(back):
    return [
        jnp.transpose(back[:, i], (1, 0, 2)).reshape(BA, 8 * WIDE) for i in range(back.shape[1])
    ]


def halo(tiles):
    up, down = routes(False)
    return lax.ppermute(tiles[1:], "vid", up), lax.ppermute(tiles[:-1], "vid", down)


def give_back(before, after):
    up, down = routes(False)
    return lax.ppermute(before, "vid", down), lax.ppermute(after, "vid", up)


def spread_low(part):
    return jnp.pad(part, ((0, 1),) + ((0, 0),) * (part.ndim - 1))


def spread_high(part):
    return jnp.pad(part, ((1, 0),) + ((0, 0),) * (part.ndim - 1))


def per_device(
    video_q,
    video_k,
    video_v,
    video_dout,
    audio_q,
    audio_k,
    audio_v,
    audio_dout,
    video_pairs,
    audio_pairs,
    video_len,
    audio_len,
):
    first = (lax.axis_index("vid") * SPAN).astype(jnp.int32).reshape(1)
    k = video_k.reshape(SPAN, BV, WIDE)
    v = video_v.reshape(SPAN, BV, WIDE)
    kc, vc = run_pack(first, video_len, k, v)
    qd = to_span(span_tiles(audio_q, audio_dout))
    kv_tiles = span_tiles(audio_k, audio_v)
    kv_tiles, kc, vc = lax.optimization_barrier((kv_tiles, kc, vc))
    qd_before, qd_after = halo(qd)
    kv = to_span(kv_tiles)
    o_own, st_own = run_part(OWN, first, audio_pairs, video_len, (qd,), kc, vc)
    kv_before, kv_after = halo(kv)

    near = (qd_before, qd_after)
    to_below, to_above, st_near = run_part(
        HALO, first, audio_pairs, video_len, near, kc, vc, st_own
    )
    st_near, audio_len = lax.optimization_barrier((st_near, audio_len))
    up, down = routes(True)
    above = lax.ppermute(to_below, "vid", down)
    below = lax.ppermute(to_above, "vid", up)

    video_out, video_dq, g_before, g_own, g_after = run_video(
        first, video_pairs, audio_len, video_q, video_dout, kv_before, kv, kv_after
    )
    g_before, g_after, above, below, later_len = lax.optimization_barrier(
        (g_before, g_after, above, below, video_len)
    )
    g_above, g_below = give_back(g_before, g_after)

    dq_before, dq_after, dq_own, out, video_dk, video_dv = run_grad(
        first, audio_pairs, later_len, near, qd, st_near, st_own, above, below, o_own, kc, vc
    )
    dq_above, dq_below = give_back(dq_before, dq_after)

    g = (g_own + spread_high(g_above).astype(F32) + spread_low(g_below).astype(F32)).astype(BF16)
    g, dq_own = lax.optimization_barrier((g, dq_own))
    g_back = to_owner(g)
    dq = (dq_own + spread_high(dq_above).astype(F32) + spread_low(dq_below).astype(F32)).astype(BF16)
    od, g_back = lax.optimization_barrier((jnp.stack([out, dq], axis=1), g_back))
    audio_dk, audio_dv = side_by_side(g_back)
    audio_out, audio_dq = side_by_side(to_owner(od))
    return (
        video_out,
        audio_out,
        video_dq,
        video_dk.reshape(video_k.shape),
        video_dv.reshape(video_k.shape),
        audio_dq,
        audio_dk,
        audio_dv,
    )


def solution(mesh):
    video = P("vid", "aud")
    audio = P(("vid", "aud"), None)
    return jax.shard_map(
        per_device,
        mesh=mesh,
        in_specs=(video,) * 4 + (audio,) * 4 + (P(),) * 4,
        out_specs=(video, audio, video, video, video, audio, audio, audio),
        check_vma=False,
    )
```
